32 devices in a mesh: groups: 1, dp: 32 (over z, y, x, core).
Axes of the slice: x: 2, y: 2, z: 4, core: 2. Of those that a mesh axis runs over, the one named last changes fastest.
Arguments:
- queries: bfloat16 [4096, 4096], P(('groups', 'dp')), may hold values from -9 to 9
- own_kv: bfloat16 [4096, 1024], P(('groups', 'dp')), may hold values from -6 to 6
- cotangent: bfloat16 [4096, 4096], P(('groups', 'dp')), may hold values from -6 to 6
- cartridges: bfloat16 [32, 768, 1024], P(('groups', 'dp')), may hold values from -6 to 6
- block_mask: int32 [32, 6], P(('groups', 'dp')), may hold values from 0 to 1, as said below
- owner: int32 [1], P('groups'), may hold values from 0 to 31
Outputs:
- update: float32 [768, 1024], P(('groups', 'dp'))
The draws below stay inside these ranges and needn't reach their ends.
Inputs may be any that keep to these rules, and one draw needn't show every extreme that they name: block_mask[c, b] is 1 when conversation c may attend to slots b * 128 to b * 128 + 127, else 0.
All inputs are finite; a program needn't handle non-finite values.
Results may differ from the reference program's by a relative error of at most 0.0047.
Values may be sent and summed in bfloat16 or wider, within the bound.
A program may use at most 64 MiB of HBM per device.

```python
import jax
import jax.numpy as jnp
from jax import lax

HD = 128
QH = 32
KVH = 4
SLOTS = 768
BLOCK = 128
LEN = 128
NBLK = 6
OWNERS = 32
CONVS = 32
TOKENS = 4096


def draw_cartridges(key, part):
    base = jax.random.fold_in(key, 11)
    shape = (OWNERS, SLOTS, 2 * KVH * HD)
    values = jnp.clip(jax.random.normal(base, shape, jnp.float32), -6.0, 6.0)
    return values.astype(jnp.bfloat16)


def draw_queries(key, part):
    base = jax.random.fold_in(key, 12)
    shape = (TOKENS, QH * HD)
    values = jnp.clip(jax.random.normal(base, shape, jnp.float32), -6.0, 6.0)
    return values.astype(jnp.bfloat16)


def draw_block_mask(key, part):
    raw = jax.random.randint(jax.random.fold_in(key, 13), (CONVS, NBLK), 0, 10)
    limit = 2 + 7 * jnp.arange(NBLK) // max(NBLK - 1, 1)
    return (raw < limit[None, :]).astype(jnp.int32)


def level_of(rng, shape, pieces, low, top_value):
    factor_of, own = 1.0, jax.random.fold_in(rng, 6)
    for position, blocks in pieces:
        steps = jnp.exp(jax.random.uniform(jax.random.fold_in(own, position), (blocks,), jnp.float32, low / len(pieces), top_value / len(pieces)))
        factor_of = factor_of * jnp.repeat(steps, shape[position] // blocks).reshape([-1 if axis == position else 1 for axis in range(len(shape))])
    return factor_of


def centred(rng, extent, deviation, most, split=(), held_as=jnp.bfloat16):
    gain = level_of(rng, extent, split, -0.22, 0.18) if split else 1.0
    array = jax.random.normal(rng, extent, jnp.float32) * deviation * gain
    return jnp.minimum(jnp.maximum(array, -most), most).astype(held_as)


def setup_inputs(seed: int = 0, part: int = 0) -> dict:
    arg_keys = jax.random.split(jax.random.key(seed), 7)
    part_keys = jax.random.split(jax.random.fold_in(arg_keys[6], part), 7)
    return {
        "queries": draw_queries(jax.random.fold_in(jax.random.fold_in(arg_keys[6], part), 71), part),
        "own_kv": centred(part_keys[1], (TOKENS, 2 * KVH * HD), 1.0, 6.0, ((0, 32),)),
        "cotangent": centred(part_keys[2], (TOKENS, QH * HD), 1.0, 6.0, ((0, 32),)),
        "cartridges": draw_cartridges(jax.random.fold_in(jax.random.fold_in(arg_keys[6], part), 71), part),
        "block_mask": draw_block_mask(jax.random.fold_in(jax.random.fold_in(arg_keys[6], part), 71), part),
        "owner": jax.random.randint(part_keys[5], (1,), 0, OWNERS).astype(jnp.int32),
    }


masked_score = -1e+30
norm_epsilon = 1e-06

def head_terms(queries, grad_out, own_keys, own_values, cart_keys, cart_values, allowed, causal):
    score_scale = HD ** (-0.5)
    query_wide = queries.astype(jnp.float32)
    grad_wide = grad_out.astype(jnp.float32)
    ckeys_wide = cart_keys.astype(jnp.float32)
    cvalues_wide = cart_values.astype(jnp.float32)
    okeys_wide = own_keys.astype(jnp.float32)
    ovalues_wide = own_values.astype(jnp.float32)
    scores_cart = jnp.einsum('clgd,sd->clgs', query_wide, ckeys_wide) * score_scale
    scores_own = jnp.einsum('clgd,cud->clgu', query_wide, okeys_wide) * score_scale
    scores_cart = jnp.where(allowed[:, None, None, :], scores_cart, masked_score)
    scores_own = jnp.where(causal[None, :, None, :], scores_own, masked_score)
    row_max = jnp.maximum(lax.optimization_barrier(jnp.max(scores_cart, axis=3)), lax.optimization_barrier(jnp.max(scores_own, axis=3)))[..., None]
    exp_cart = jnp.exp(scores_cart - row_max)
    exp_own = jnp.exp(scores_own - row_max)
    row_sum = lax.optimization_barrier(jnp.sum(exp_cart, axis=3, keepdims=True)) + lax.optimization_barrier(jnp.sum(exp_own, axis=3, keepdims=True))
    prob_cart = exp_cart / row_sum
    prob_own = exp_own / row_sum
    low_cart = lax.optimization_barrier(prob_cart.astype(jnp.bfloat16)).astype(jnp.float32)
    low_own = lax.optimization_barrier(prob_own.astype(jnp.bfloat16)).astype(jnp.float32)
    attended = jnp.einsum('clgs,sd->clgd', low_cart, cvalues_wide) + jnp.einsum('clgu,cud->clgd', low_own, ovalues_wide)
    grad_prob = jnp.einsum('clgd,sd->clgs', grad_wide, cvalues_wide)
    row_dot = lax.optimization_barrier(jnp.sum(grad_wide * attended, axis=3, keepdims=True))
    grad_score = prob_cart * (grad_prob - row_dot)
    grad_score = lax.optimization_barrier(grad_score.astype(jnp.bfloat16)).astype(jnp.float32)
    grad_keys = jnp.einsum('clgs,clgd->sd', grad_score, query_wide) * score_scale
    grad_values = jnp.einsum('clgs,clgd->sd', low_cart, grad_wide)
    return (grad_keys, grad_values)

def reference(queries, own_kv, cotangent, cartridges, block_mask, owner):
    cart = lax.dynamic_index_in_dim(cartridges, owner[0].astype(jnp.int32), 0, keepdims=False)
    convs = block_mask.shape[0]
    groups_q = QH // KVH
    key_heads = cart[:, :KVH * HD].reshape(SLOTS, KVH, HD)
    value_heads = cart[:, KVH * HD:].reshape(SLOTS, KVH, HD)
    query_heads = queries.reshape(convs, LEN, KVH, groups_q, HD)
    grad_heads = cotangent.reshape(convs, LEN, KVH, groups_q, HD)
    own_heads = own_kv.reshape(convs, LEN, 2, KVH, HD)
    allowed = jnp.repeat(block_mask > 0, BLOCK, axis=1)
    positions = jnp.arange(LEN)
    causal = positions[:, None] >= positions[None, :]

    def one_conversation(running, items):
        query_one, grad_one, own_one, allow_one = items
        key_parts = []
        value_parts = []
        for kv_head in range(KVH):
            keys_part, values_part = head_terms(query_one[None, :, kv_head], grad_one[None, :, kv_head], own_one[None, :, 0, kv_head], own_one[None, :, 1, kv_head], key_heads[:, kv_head], value_heads[:, kv_head], allow_one[None], causal)
            key_parts.append(keys_part)
            value_parts.append(values_part)
        return (running + jnp.concatenate(key_parts + value_parts, axis=1), None)
    start_grad = jnp.zeros((SLOTS, 2 * KVH * HD), jnp.float32)
    grad_total, _ = lax.scan(one_conversation, start_grad, (query_heads, grad_heads, own_heads, allowed))
    return grad_total / jnp.sqrt(jnp.mean(grad_total * grad_total) + norm_epsilon)
```

```python
import jax
import jax.numpy as jnp
from jax import lax
from jax.experimental import pallas as pl
from jax.experimental.pallas import tpu as pltpu
from jax.sharding import PartitionSpec as P

HD = 128
QH = 32
KVH = 4
BLOCK = 128


masked_score = -1e30
norm_epsilon = 1e-06


def from_root(value, axis, source):
    kept = jnp.where(lax.axis_index(axis) == source, value, 0).astype(value.dtype)
    return lax.psum(kept, axis)


def head_terms(queries, grad_out, own_keys, own_values, cart_keys, cart_values, allowed, causal):
    score_scale = HD ** (-0.5)
    scores_cart = (
        jnp.einsum("clgd,sd->clgs", queries, cart_keys, preferred_element_type=jnp.float32)
        * score_scale
    )
    scores_own = (
        jnp.einsum("clgd,cud->clgu", queries, own_keys, preferred_element_type=jnp.float32)
        * score_scale
    )
    scores_cart = jnp.where(allowed[:, None, None, :], scores_cart, masked_score)
    scores_own = jnp.where(causal[None, :, None, :], scores_own, masked_score)
    row_max = jnp.maximum(jnp.max(scores_cart, axis=3), jnp.max(scores_own, axis=3))[..., None]
    exp_cart = jnp.exp(scores_cart - row_max)
    exp_own = jnp.exp(scores_own - row_max)
    row_sum = jnp.sum(exp_cart, axis=3, keepdims=True) + jnp.sum(exp_own, axis=3, keepdims=True)
    prob_cart = exp_cart / row_sum
    prob_own = exp_own / row_sum
    low_cart = prob_cart.astype(jnp.bfloat16)
    low_own = prob_own.astype(jnp.bfloat16)
    attended = jnp.einsum(
        "clgs,sd->clgd", low_cart, cart_values, preferred_element_type=jnp.float32
    )
    attended = attended + jnp.einsum(
        "clgu,cud->clgd", low_own, own_values, preferred_element_type=jnp.float32
    )
    grad_prob = jnp.einsum(
        "clgd,sd->clgs", grad_out, cart_values, preferred_element_type=jnp.float32
    )
    row_dot = jnp.sum(grad_out.astype(jnp.float32) * attended, axis=3, keepdims=True)
    grad_score = (prob_cart * (grad_prob - row_dot)).astype(jnp.bfloat16)
    grad_keys = (
        jnp.einsum("clgs,clgd->sd", grad_score, queries, preferred_element_type=jnp.float32)
        * score_scale
    )
    grad_values = jnp.einsum(
        "clgs,clgd->sd", low_cart, grad_out, preferred_element_type=jnp.float32
    )
    return (grad_keys, grad_values)


def body(queries, own_kv, cotangent, cartridges, block_mask, owner):
    conv_dev = block_mask.shape[0]
    seq_len = queries.shape[0] // conv_dev
    slot_count = cartridges.shape[1]
    half_width = KVH * HD
    groups_q = QH // KVH
    owner_index = owner[0]
    local_cart = cartridges[0]
    whole_cart = from_root(local_cart, "dp", owner_index)
    cart_keys = whole_cart[:, :half_width]
    cart_values = whole_cart[:, half_width:]
    query_heads = queries.reshape(conv_dev, seq_len, KVH, groups_q, HD)
    grad_heads = cotangent.reshape(conv_dev, seq_len, KVH, groups_q, HD)
    own_heads = own_kv.reshape(conv_dev, seq_len, 2, KVH, HD)
    key_heads = cart_keys.reshape(slot_count, KVH, HD)
    value_heads = cart_values.reshape(slot_count, KVH, HD)
    allowed = jnp.repeat(block_mask > 0, BLOCK, axis=1)
    positions = jnp.arange(seq_len)
    causal = positions[:, None] >= positions[None, :]
    key_parts = []
    value_parts = []
    for kv_head in range(KVH):
        keys_part, values_part = head_terms(
            query_heads[:, :, kv_head],
            grad_heads[:, :, kv_head],
            own_heads[:, :, 0, kv_head],
            own_heads[:, :, 1, kv_head],
            key_heads[:, kv_head],
            value_heads[:, kv_head],
            allowed,
            causal,
        )
        key_parts.append(keys_part)
        value_parts.append(values_part)
    local_grad = jnp.concatenate(key_parts + value_parts, axis=1)
    width_total = local_grad.shape[1]
    own_rows = lax.psum_scatter(local_grad, "dp", scatter_dimension=0, tiled=True)
    squares = lax.psum(jnp.sum(own_rows * own_rows), "dp")
    return own_rows / jnp.sqrt(squares / (slot_count * width_total) + norm_epsilon)


SCALE = HD ** (-0.5)
LOG2E = 1.4426950408889634


def attend(j, q_ref, kv_ref, ct_ref, bias_ref, cart, kk, vv, grad):
    slots = SLOTS_PER
    half = KVH * HD
    kk[:slots] = cart[j, :, :, :, 0].reshape(slots, HD)
    vv[:slots] = cart[j, :, :, :, 1].reshape(slots, HD)
    kk[slots:] = kv_ref[:, j * HD:(j + 1) * HD]
    vv[slots:] = kv_ref[:, half + j * HD:half + (j + 1) * HD]
    groups = QH // KVH
    grad[j] = jnp.zeros_like(grad[j])

    def pair(i, carry):
        base = j * groups * HD + i * 2 * HD
        one = pl.ds(pl.multiple_of(base, HD), HD)
        two = pl.ds(pl.multiple_of(base + HD, HD), HD)
        q = jnp.concatenate([q_ref[:, one], q_ref[:, two]], axis=0)
        ct = jnp.concatenate([ct_ref[:, one], ct_ref[:, two]], axis=0)
        nt = (((1,), (1,)), ((), ()))
        scores = lax.dot_general(kk[...], q, nt, preferred_element_type=jnp.float32)
        x = scores * (SCALE * LOG2E) + bias_ref[...]
        e = jnp.exp2(x - jnp.max(x, axis=0, keepdims=True))
        prob = e * (1.0 / jnp.sum(e, axis=0, keepdims=True))
        low = prob.astype(jnp.bfloat16)
        gp = lax.dot_general(vv[...], ct, nt, preferred_element_type=jnp.float32)
        row_dot = jnp.sum(low.astype(jnp.float32) * gp, axis=0, keepdims=True)
        gs = (prob[:slots] * (gp[:slots] - row_dot)).astype(jnp.bfloat16)
        grad[j, :, :HD] += jnp.dot(gs, q, preferred_element_type=jnp.float32)
        grad[j, :, HD:] += jnp.dot(low[:slots], ct, preferred_element_type=jnp.float32)
        return carry

    lax.fori_loop(0, groups // 2, pair, 0)
    grad[j, :, :HD] = grad[j, :, :HD] * SCALE


SLOTS_PER = 768
SEG = (24, 2 * HD)
N_SEM = 21 * KVH + 7


def kernel(q_ref, kv_ref, ct_ref, bias_ref, w_ref, out_ref,
           cart, rc, a1, rx, a2, rz, kk, vv, grad,
           gc, b1, sx, gx, b2, gz, own, sq, sqr, send_sem, recv_sem):
    me = lax.axis_index("dp")
    core = me % 2
    xy = (me // 2) % 4
    zz = me // 8
    bit = [me % 2, (me // 2) % 2, (me // 4) % 2, (me // 8) % 2, (me // 16) % 2]
    flip = [1 - 2 * b for b in bit]

    def moved(d, lo):
        step = 0
        if d & 1:
            step = step + flip[lo]
        if d & 2:
            step = step + 2 * flip[lo + 1]
        return step

    core_peer = me + flip[0]
    xy_step = {d: moved(d, 1) for d in (1, 2, 3)}
    z_step = {d: moved(d, 3) for d in (1, 2, 3)}
    xy_peer = {d: me + 2 * xy_step[d] for d in (1, 2, 3)}
    z_peer = {d: me + 8 * z_step[d] for d in (1, 2, 3)}

    barrier = pltpu.get_barrier_semaphore()
    peers = [core_peer] + list(xy_peer.values()) + list(z_peer.values())
    for peer in peers:
        pl.semaphore_signal(barrier, inc=1, device_id={"dp": peer}, device_id_type=pl.DeviceIdType.MESH)
    pl.semaphore_wait(barrier, len(peers))

    sent = []
    count = [0]

    def send(src, dst, peer):
        i = count[0]
        count[0] += 1
        copy = pltpu.make_async_remote_copy(
            src_ref=src, dst_ref=dst, send_sem=send_sem.at[i], recv_sem=recv_sem.at[i],
            device_id={"dp": peer}, device_id_type=pl.DeviceIdType.MESH)
        copy.start()
        sent.append(copy)
        return copy

    def head(j):
        c = [send(w_ref.at[j, 1 - core], rc.at[j], core_peer)]
        yield
        c[0].wait_recv()
        a1[j] = w_ref[j, core] + rc[j]
        c = [send(a1.at[j, xy + xy_step[d]], rx.at[j, d - 1], xy_peer[d]) for d in (1, 2, 3)]
        yield
        for k in c:
            k.wait_recv()
        a2[j] = (a1[j, xy] + rx[j, 0]) + (rx[j, 1] + rx[j, 2])
        c = []
        for d in (1, 2, 3):
            p = zz + z_step[d]
            c.append(send(a2.at[j, p // 2, p % 2], rz.at[j, d - 1], z_peer[d]))
        yield
        for k in c:
            k.wait_recv()
        spot = cart.at[j, core, xy, zz // 2, zz % 2]
        cart[j, core, xy, zz // 2, zz % 2] = (a2[j, zz // 2, zz % 2] + rz[j, 0]) + (rz[j, 1] + rz[j, 2])
        c = [send(spot, spot, z_peer[d]) for d in (1, 2, 3)]
        yield
        for k in c:
            k.wait_recv()
        spot = cart.at[j, core, xy]
        c = [send(spot, spot, xy_peer[d]) for d in (1, 2, 3)]
        yield
        for k in c:
            k.wait_recv()
        c = [send(cart.at[j, core], cart.at[j, core], core_peer)]
        yield
        c[0].wait_recv()
        yield "compute"
        attend(j, q_ref, kv_ref, ct_ref, bias_ref, cart, kk, vv, grad)
        half = SLOTS_PER // 2
        c = [send(grad.at[j, pl.ds(pl.multiple_of((1 - core) * half, 8), half)], gc.at[j], core_peer)]
        yield
        c[0].wait_recv()
        b1[j] = (grad[j, pl.ds(pl.multiple_of(core * half, 8), half)] + gc[j]).reshape(4, half // 4, 2 * HD)
        c = []
        for d in (1, 2, 3):
            sx[j, d - 1] = b1[j, xy + xy_step[d]].astype(jnp.bfloat16)
            c.append(send(sx.at[j, d - 1], gx.at[j, d - 1], xy_peer[d]))
        yield
        for k in c:
            k.wait_recv()
        total = b1[j, xy]
        for d in (1, 2, 3):
            total = total + gx[j, d - 1].astype(jnp.float32)
        b2[j] = total.reshape(4, SEG[0], SEG[1])
        c = [send(b2.at[j, zz + z_step[d]], gz.at[j, d - 1], z_peer[d]) for d in (1, 2, 3)]
        yield
        for k in c:
            k.wait_recv()
        own[j] = (b2[j, zz] + gz[j, 0]) + (gz[j, 1] + gz[j, 2])

    heads = [head(j) for j in range(KVH)]
    started = 0
    waiting = {}
    tick = 0
    live = []
    while True:
        if started < KVH:
            live.append(started)
            started += 1
        if not live:
            break
        ready = None
        for j in list(live):
            if j in waiting:
                continue
            try:
                got = next(heads[j])
                if got == "compute":
                    waiting[j] = True
            except StopIteration:
                live.remove(j)
        if waiting:
            j = min(waiting)
            del waiting[j]
            next(heads[j])
        tick += 1

    part = jnp.zeros((8, HD), jnp.float32)
    for j in range(KVH):
        v = own[j]
        v = v * v
        for r in range(0, SEG[0], 8):
            for l in range(0, SEG[1], HD):
                part = part + v[r:r + 8, l:l + HD]
    sq[0] = part
    c = send(sq.at[0], sqr.at[0], core_peer)
    c.wait_recv()
    sq[1] = sq[0] + sqr[0]
    cs = [send(sq.at[1], sqr.at[d], xy_peer[d]) for d in (1, 2, 3)]
    for k in cs:
        k.wait_recv()
    sq[2] = (sq[1] + sqr[1]) + (sqr[2] + sqr[3])
    cs = [send(sq.at[2], sqr.at[3 + d], z_peer[d]) for d in (1, 2, 3)]
    for k in cs:
        k.wait_recv()
    squares = jnp.sum((sq[2] + sqr[4]) + (sqr[5] + sqr[6]))
    factor = 1.0 / jnp.sqrt(squares * jnp.ones((1, HD), jnp.float32) / (SLOTS_PER * 2 * KVH * HD) + norm_epsilon)
    for j in range(KVH):
        out_ref[:, j * HD:(j + 1) * HD] = own[j, :, :HD] * factor
        out_ref[:, (KVH + j) * HD:(KVH + j + 1) * HD] = own[j, :, HD:] * factor
    for k in sent:
        k.wait_send()


def fused(queries, own_kv, cotangent, cartridges, block_mask, owner):
    slots, width = cartridges.shape[1:]
    seq = queries.shape[0]
    mine = jnp.where(lax.axis_index("dp") == owner[0], cartridges[0], 0).astype(jnp.bfloat16)
    w = mine.reshape(4, 4, 2, 24, 2, KVH, HD).transpose(5, 2, 1, 0, 3, 4, 6)
    w = w.reshape(KVH, 2, 4, 2, 48, 2, HD).transpose(0, 1, 2, 3, 5, 4, 6)
    allowed = jnp.repeat(block_mask[0] > 0, BLOCK)
    allowed = allowed.reshape(4, 4, 2, 24).transpose(2, 1, 0, 3).reshape(slots)
    bias = jnp.broadcast_to(jnp.where(allowed, 0.0, masked_score)[:, None], (slots, 2 * seq))
    pos = jnp.arange(seq)
    causal = jnp.where(pos[:, None] <= jnp.tile(pos, 2)[None, :], 0.0, masked_score)
    bias = jnp.concatenate([bias, causal], axis=0).astype(jnp.float32)
    bf, f32 = jnp.bfloat16, jnp.float32
    vm = pl.BlockSpec(memory_space=pltpu.VMEM)
    piece = (48, HD)
    return pl.pallas_call(
        kernel,
        out_shape=jax.ShapeDtypeStruct((24, width), f32),
        in_specs=[vm] * 5,
        out_specs=vm,
        scratch_shapes=[
            pltpu.VMEM((KVH, 2, 4, 2, 2) + piece, bf),
            pltpu.VMEM((KVH, 4, 2, 2) + piece, bf),
            pltpu.VMEM((KVH, 4, 2, 2) + piece, bf),
            pltpu.VMEM((KVH, 3, 2, 2) + piece, bf),
            pltpu.VMEM((KVH, 2, 2) + piece, bf),
            pltpu.VMEM((KVH, 3) + piece, bf),
            pltpu.VMEM((slots + seq, HD), bf),
            pltpu.VMEM((slots + seq, HD), bf),
            pltpu.VMEM((KVH, slots, 2 * HD), f32),
            pltpu.VMEM((KVH, slots // 2, 2 * HD), f32),
            pltpu.VMEM((KVH, 4, slots // 8, 2 * HD), f32),
            pltpu.VMEM((KVH, 3, slots // 8, 2 * HD), bf),
            pltpu.VMEM((KVH, 3, slots // 8, 2 * HD), bf),
            pltpu.VMEM((KVH, 4) + SEG, f32),
            pltpu.VMEM((KVH, 3) + SEG, f32),
            pltpu.VMEM((KVH,) + SEG, f32),
            pltpu.VMEM((3, 8, HD), f32),
            pltpu.VMEM((7, 8, HD), f32),
            pltpu.SemaphoreType.DMA((N_SEM,)),
            pltpu.SemaphoreType.DMA((N_SEM,)),
        ],
        compiler_params=pltpu.CompilerParams(
            collective_id=0, has_side_effects=True, vmem_limit_bytes=48 * 1024 * 1024),
    )(queries, own_kv, cotangent, bias, w)


def dispatch(size):
    def run(queries, own_kv, cotangent, cartridges, block_mask, owner):
        fits = (size == 32 and block_mask.shape == (1, 6)
                and queries.shape == (128, QH * HD)
                and cartridges.shape == (1, SLOTS_PER, 2 * KVH * HD))
        chosen = fused if fits else body
        return chosen(queries, own_kv, cotangent, cartridges, block_mask, owner)
    return run


def solution(mesh):
    return jax.shard_map(
        dispatch(mesh.shape["dp"]),
        mesh=mesh,
        in_specs=(
            P(("groups", "dp"), None),
            P(("groups", "dp"), None),
            P(("groups", "dp"), None),
            P(("groups", "dp"), None, None),
            P(("groups", "dp"), None),
            P("groups"),
        ),
        out_specs=P(("groups", "dp"), None),
        check_vma=False,
    )
```

```python
import jax
import jax.numpy as jnp
from jax import lax
from jax.experimental import pallas as pl
from jax.experimental.pallas import tpu as pltpu
from jax.sharding import PartitionSpec as P

HD = 128
QH = 32
KVH = 4
BLOCK = 128


masked_score = -1e30
norm_epsilon = 1e-06


def from_root(value, axis, source):
    kept = jnp.where(lax.axis_index(axis) == source, value, 0).astype(value.dtype)
    return lax.psum(kept, axis)


def head_terms(queries, grad_out, own_keys, own_values, cart_keys, cart_values, allowed, causal):
    score_scale = HD ** (-0.5)
    scores_cart = (
        jnp.einsum("clgd,sd->clgs", queries, cart_keys, preferred_element_type=jnp.float32)
        * score_scale
    )
    scores_own = (
        jnp.einsum("clgd,cud->clgu", queries, own_keys, preferred_element_type=jnp.float32)
        * score_scale
    )
    scores_cart = jnp.where(allowed[:, None, None, :], scores_cart, masked_score)
    scores_own = jnp.where(causal[None, :, None, :], scores_own, masked_score)
    row_max = jnp.maximum(jnp.max(scores_cart, axis=3), jnp.max(scores_own, axis=3))[..., None]
    exp_cart = jnp.exp(scores_cart - row_max)
    exp_own = jnp.exp(scores_own - row_max)
    row_sum = jnp.sum(exp_cart, axis=3, keepdims=True) + jnp.sum(exp_own, axis=3, keepdims=True)
    prob_cart = exp_cart / row_sum
    prob_own = exp_own / row_sum
    low_cart = prob_cart.astype(jnp.bfloat16)
    low_own = prob_own.astype(jnp.bfloat16)
    attended = jnp.einsum(
        "clgs,sd->clgd", low_cart, cart_values, preferred_element_type=jnp.float32
    )
    attended = attended + jnp.einsum(
        "clgu,cud->clgd", low_own, own_values, preferred_element_type=jnp.float32
    )
    grad_prob = jnp.einsum(
        "clgd,sd->clgs", grad_out, cart_values, preferred_element_type=jnp.float32
    )
    row_dot = jnp.sum(grad_out.astype(jnp.float32) * attended, axis=3, keepdims=True)
    grad_score = (prob_cart * (grad_prob - row_dot)).astype(jnp.bfloat16)
    grad_keys = (
        jnp.einsum("clgs,clgd->sd", grad_score, queries, preferred_element_type=jnp.float32)
        * score_scale
    )
    grad_values = jnp.einsum(
        "clgs,clgd->sd", low_cart, grad_out, preferred_element_type=jnp.float32
    )
    return (grad_keys, grad_values)


def body(queries, own_kv, cotangent, cartridges, block_mask, owner):
    conv_dev = block_mask.shape[0]
    seq_len = queries.shape[0] // conv_dev
    slot_count = cartridges.shape[1]
    half_width = KVH * HD
    groups_q = QH // KVH
    owner_index = owner[0]
    local_cart = cartridges[0]
    whole_cart = from_root(local_cart, "dp", owner_index)
    cart_keys = whole_cart[:, :half_width]
    cart_values = whole_cart[:, half_width:]
    query_heads = queries.reshape(conv_dev, seq_len, KVH, groups_q, HD)
    grad_heads = cotangent.reshape(conv_dev, seq_len, KVH, groups_q, HD)
    own_heads = own_kv.reshape(conv_dev, seq_len, 2, KVH, HD)
    key_heads = cart_keys.reshape(slot_count, KVH, HD)
    value_heads = cart_values.reshape(slot_count, KVH, HD)
    allowed = jnp.repeat(block_mask > 0, BLOCK, axis=1)
    positions = jnp.arange(seq_len)
    causal = positions[:, None] >= positions[None, :]
    key_parts = []
    value_parts = []
    for kv_head in range(KVH):
        keys_part, values_part = head_terms(
            query_heads[:, :, kv_head],
            grad_heads[:, :, kv_head],
            own_heads[:, :, 0, kv_head],
            own_heads[:, :, 1, kv_head],
            key_heads[:, kv_head],
            value_heads[:, kv_head],
            allowed,
            causal,
        )
        key_parts.append(keys_part)
        value_parts.append(values_part)
    local_grad = jnp.concatenate(key_parts + value_parts, axis=1)
    width_total = local_grad.shape[1]
    own_rows = lax.psum_scatter(local_grad, "dp", scatter_dimension=0, tiled=True)
    squares = lax.psum(jnp.sum(own_rows * own_rows), "dp")
    return own_rows / jnp.sqrt(squares / (slot_count * width_total) + norm_epsilon)


SCALE = HD ** (-0.5)
LOG2E = 1.4426950408889634


PAIRS = 1
SLICES = 2
LAT = 2.2
COST = 3.0


def attend_begin(j, kv_ref, cart, kk, vv):
    slots = SLOTS_PER
    half = KVH * HD
    kk[:slots] = cart[j, :, :, :, 0].reshape(slots, HD)
    vv[:slots] = cart[j, :, :, :, 1].reshape(slots, HD)
    kk[slots:] = kv_ref[:, j * HD:(j + 1) * HD]
    vv[slots:] = kv_ref[:, half + j * HD:half + (j + 1) * HD]


def attend_slice(j, part, q_ref, ct_ref, bias_ref, kk, vv, acc):
    slots = SLOTS_PER
    groups = QH // KVH
    wide = groups // SLICES // PAIRS * HD
    nt = (((1,), (1,)), ((), ()))
    for i in range(PAIRS):
        base = (j * groups) * HD + (part * PAIRS + i) * wide
        cols = [slice(base + h, base + h + HD) for h in range(0, wide, HD)]
        q = jnp.concatenate([q_ref[:, c] for c in cols], axis=0)
        ct = jnp.concatenate([ct_ref[:, c] for c in cols], axis=0)
        scores = lax.dot_general(kk[...], q, nt, preferred_element_type=jnp.float32)
        x = scores * (SCALE * LOG2E) + bias_ref[:, :wide]
        e = jnp.exp2(x - jnp.max(x, axis=0, keepdims=True))
        prob = e * (1.0 / jnp.sum(e, axis=0, keepdims=True))
        low = prob.astype(jnp.bfloat16)
        gp = lax.dot_general(vv[...], ct, nt, preferred_element_type=jnp.float32)
        row_dot = jnp.sum(low.astype(jnp.float32) * gp, axis=0, keepdims=True)
        gs = (prob[:slots] * (gp[:slots] - row_dot)).astype(jnp.bfloat16)
        gk = jnp.dot(gs, q, preferred_element_type=jnp.float32)
        gv = jnp.dot(low[:slots], ct, preferred_element_type=jnp.float32)
        if part + i == 0:
            acc[:, :HD] = gk
            acc[:, HD:] = gv
        else:
            acc[:, :HD] += gk
            acc[:, HD:] += gv


def attend_end(j, acc, grad):
    for z in range(4):
        for xy in range(4):
            for c in range(2):
                row = 24 * ((z * 4 + xy) * 2 + c)
                to = 24 * ((c * 4 + xy) * 4 + z)
                grad[j, to:to + 24, :HD] = acc[row:row + 24, :HD] * SCALE
                grad[j, to:to + 24, HD:] = acc[row:row + 24, HD:]


SLOTS_PER = 768
SEG = (24, 2 * HD)
N_SEM = 21 * KVH + 10


def kernel(q_hbm, kv_hbm, ct_hbm, own_cart, mask_ref, owner_ref, out_ref,
           q_ref, kv_ref, ct_ref, load_sem, bias_ref, w_ref, acc, cart, rc, a1, rx, a2, rz, kk, vv, grad,
           gc, b1, sx, gx, b2, gz, own, sq, sqr, send_sem, recv_sem):
    me = lax.axis_index("dp")
    core = me % 2
    xy = (me // 2) % 4
    zz = me // 8
    bit = [me % 2, (me // 2) % 2, (me // 4) % 2, (me // 8) % 2, (me // 16) % 2]
    flip = [1 - 2 * b for b in bit]

    def moved(d, lo):
        step = 0
        if d & 1:
            step = step + flip[lo]
        if d & 2:
            step = step + 2 * flip[lo + 1]
        return step

    core_peer = me + flip[0]
    xy_step = {d: moved(d, 1) for d in (1, 2, 3)}
    z_step = {d: moved(d, 3) for d in (1, 2, 3)}
    xy_peer = {d: me + 2 * xy_step[d] for d in (1, 2, 3)}
    z_peer = {d: me + 8 * z_step[d] for d in (1, 2, 3)}

    barrier = pltpu.get_barrier_semaphore()
    every = {d: me + moved(d % 2, 0) + 2 * moved(d // 2 % 4, 1) + 8 * moved(d // 8, 3) for d in range(1, 32)}
    peers = [every[d] for d in range(1, 8)] + list(z_peer.values())
    for peer in peers:
        pl.semaphore_signal(barrier, inc=1, device_id={"dp": peer}, device_id_type=pl.DeviceIdType.MESH)

    staged = [pltpu.make_async_copy(src, dst, load_sem.at[i])
              for i, (src, dst) in enumerate([(q_hbm, q_ref), (ct_hbm, ct_ref), (kv_hbm, kv_ref)])]
    for copy in staged:
        copy.start()
    mine = owner_ref[0] == me
    for j in range(KVH):
        for c in range(2):
            for p in range(4):
                for r in range(2):
                    row = c * 384 + p * 96 + r * 48
                    for v in range(2):
                        col = (v * KVH + j) * HD
                        w_ref[j, c, p, r, v] = jnp.where(mine, own_cart[0, row:row + 48, col:col + HD], 0).astype(jnp.bfloat16)
    for u in range(0, SLOTS_PER, BLOCK):
        bias_ref[u:u + BLOCK] = jnp.full((BLOCK, bias_ref.shape[1]), jnp.where(mask_ref[0, u // BLOCK] > 0, 0.0, masked_score), jnp.float32)
    own_pos = lax.broadcasted_iota(jnp.int32, (BLOCK, bias_ref.shape[1]), 0)
    row_pos = lax.broadcasted_iota(jnp.int32, (BLOCK, bias_ref.shape[1]), 1) % BLOCK
    bias_ref[SLOTS_PER:] = jnp.where(own_pos <= row_pos, 0.0, masked_score)
    pl.semaphore_wait(barrier, len(peers))
    sent = []
    count = [0]

    def send(src, dst, peer):
        i = count[0]
        count[0] += 1
        copy = pltpu.make_async_remote_copy(
            src_ref=src, dst_ref=dst, send_sem=send_sem.at[i], recv_sem=recv_sem.at[i],
            device_id={"dp": peer}, device_id_type=pl.DeviceIdType.MESH)
        copy.start()
        sent.append(copy)
        return copy

    def head(j):
        c = [send(w_ref.at[j, 1 - core], rc.at[j], core_peer)]
        yield ("c", 0.5)
        c[0].wait_recv()
        a1[j] = w_ref[j, core] + rc[j]
        c = [send(a1.at[j, xy + xy_step[d]], rx.at[j, d - 1], xy_peer[d]) for d in (1, 2, 3)]
        yield ("x", 2.0)
        for k in c:
            k.wait_recv()
        a2[j] = (a1[j, xy] + rx[j, 0]) + (rx[j, 1] + rx[j, 2])
        c = []
        for d in (1, 2, 3):
            p = zz + z_step[d]
            c.append(send(a2.at[j, p // 2, p % 2], rz.at[j, d - 1], z_peer[d]))
        yield ("z", 1.0)
        for k in c:
            k.wait_recv()
        spot = cart.at[j, core, xy, zz // 2, zz % 2]
        cart[j, core, xy, zz // 2, zz % 2] = (a2[j, zz // 2, zz % 2] + rz[j, 0]) + (rz[j, 1] + rz[j, 2])
        c = [send(spot, spot, z_peer[d]) for d in (1, 2, 3)]
        yield ("z", 1.0)
        for k in c:
            k.wait_recv()
        spot = cart.at[j, core, xy]
        c = [send(spot, spot, xy_peer[d]) for d in (1, 2, 3)]
        yield ("x", 2.0)
        for k in c:
            k.wait_recv()
        c = [send(cart.at[j, core], cart.at[j, core], core_peer)]
        yield ("c", 0.5)
        c[0].wait_recv()
        yield "compute"
        attend_begin(j, kv_ref, cart, kk, vv)
        for part in range(SLICES):
            attend_slice(j, part, q_ref, ct_ref, bias_ref, kk, vv, acc)
            if part < SLICES - 1:
                yield "compute"
        attend_end(j, acc, grad)
        half = SLOTS_PER // 2
        c = [send(grad.at[j, pl.ds(pl.multiple_of((1 - core) * half, 8), half)], gc.at[j], core_peer)]
        yield ("c", 0.8)
        c[0].wait_recv()
        b1[j] = (grad[j, pl.ds(pl.multiple_of(core * half, 8), half)] + gc[j]).reshape(4, half // 4, 2 * HD)
        c = []
        for d in (1, 2, 3):
            sx[j, d - 1] = b1[j, xy + xy_step[d]].astype(jnp.bfloat16)
            c.append(send(sx.at[j, d - 1], gx.at[j, d - 1], xy_peer[d]))
        yield ("x", 2.0)
        for k in c:
            k.wait_recv()
        total = b1[j, xy]
        for d in (1, 2, 3):
            total = total + gx[j, d - 1].astype(jnp.float32)
        b2[j] = total.reshape(4, SEG[0], SEG[1])
        c = [send(b2.at[j, zz + z_step[d]], gz.at[j, d - 1], z_peer[d]) for d in (1, 2, 3)]
        yield ("z", 2.0)
        for k in c:
            k.wait_recv()
        own[j] = (b2[j, zz] + gz[j, 0]) + (gz[j, 1] + gz[j, 2])

    heads = [head(j) for j in range(KVH)]
    link = {"c": 0.0, "x": 0.0, "z": 0.0}
    now = 0.0
    ready = {}
    computing = []

    def advance(j):
        got = next(heads[j], None)
        ready.pop(j, None)
        if got == "compute":
            computing.append(j)
        elif got is not None:
            name, cost = got
            link[name] = max(link[name], now) + cost
            ready[j] = link[name] + LAT

    for j in range(KVH):
        advance(j)
    for copy in staged:
        copy.wait()
    while ready or computing:
        arrived = [j for j in sorted(ready) if ready[j] <= now]
        if arrived:
            now += 0.15
            advance(arrived[0])
        elif computing:
            j = min(computing)
            computing.remove(j)
            now += COST / SLICES
            advance(j)
        else:
            now = min(ready.values())

    part = jnp.zeros((8, HD), jnp.float32)
    for j in range(KVH):
        v = own[j]
        v = v * v
        for r in range(0, SEG[0], 8):
            for l in range(0, SEG[1], HD):
                part = part + v[r:r + 8, l:l + HD]
    sq[0] = part
    eight = {d: every[d] for d in range(1, 8)}
    cs = [send(sq.at[0], sqr.at[d - 1], eight[d]) for d in range(1, 8)]
    for k in cs:
        k.wait_recv()
    sq[1] = (((sq[0] + sqr[0]) + (sqr[1] + sqr[2])) + ((sqr[3] + sqr[4]) + (sqr[5] + sqr[6])))
    cs = [send(sq.at[1], sqr.at[6 + d], z_peer[d]) for d in (1, 2, 3)]
    for k in cs:
        k.wait_recv()
    squares = jnp.sum((sq[1] + sqr[7]) + (sqr[8] + sqr[9]))
    factor = 1.0 / jnp.sqrt(squares * jnp.ones((1, HD), jnp.float32) / (SLOTS_PER * 2 * KVH * HD) + norm_epsilon)
    for j in range(KVH):
        out_ref[:, j * HD:(j + 1) * HD] = own[j, :, :HD] * factor
        out_ref[:, (KVH + j) * HD:(KVH + j + 1) * HD] = own[j, :, HD:] * factor
    for k in sent:
        k.wait_send()


def fused(queries, own_kv, cotangent, cartridges, block_mask, owner):
    slots, width = cartridges.shape[1:]
    seq = queries.shape[0]
    bf, f32 = jnp.bfloat16, jnp.float32
    vm = pl.BlockSpec(memory_space=pltpu.VMEM)
    sm = pl.BlockSpec(memory_space=pltpu.SMEM)
    piece = (48, HD)
    return pl.pallas_call(
        kernel,
        out_shape=jax.ShapeDtypeStruct((24, width), f32),
        in_specs=[pl.BlockSpec(memory_space=pl.ANY)] * 3 + [vm] + [sm] * 2,
        out_specs=vm,
        scratch_shapes=[
            pltpu.VMEM(queries.shape, bf),
            pltpu.VMEM(own_kv.shape, bf),
            pltpu.VMEM(cotangent.shape, bf),
            pltpu.SemaphoreType.DMA((3,)),
            pltpu.VMEM((slots + seq, QH // KVH // SLICES // PAIRS * HD), f32),
            pltpu.VMEM((KVH, 2, 4, 2, 2) + piece, bf),
            pltpu.VMEM((slots, 2 * HD), f32),
            pltpu.VMEM((KVH, 2, 4, 2, 2) + piece, bf),
            pltpu.VMEM((KVH, 4, 2, 2) + piece, bf),
            pltpu.VMEM((KVH, 4, 2, 2) + piece, bf),
            pltpu.VMEM((KVH, 3, 2, 2) + piece, bf),
            pltpu.VMEM((KVH, 2, 2) + piece, bf),
            pltpu.VMEM((KVH, 3) + piece, bf),
            pltpu.VMEM((slots + seq, HD), bf),
            pltpu.VMEM((slots + seq, HD), bf),
            pltpu.VMEM((KVH, slots, 2 * HD), f32),
            pltpu.VMEM((KVH, slots // 2, 2 * HD), f32),
            pltpu.VMEM((KVH, 4, slots // 8, 2 * HD), f32),
            pltpu.VMEM((KVH, 3, slots // 8, 2 * HD), bf),
            pltpu.VMEM((KVH, 3, slots // 8, 2 * HD), bf),
            pltpu.VMEM((KVH, 4) + SEG, f32),
            pltpu.VMEM((KVH, 3) + SEG, f32),
            pltpu.VMEM((KVH,) + SEG, f32),
            pltpu.VMEM((2, 8, HD), f32),
            pltpu.VMEM((10, 8, HD), f32),
            pltpu.SemaphoreType.DMA((N_SEM,)),
            pltpu.SemaphoreType.DMA((N_SEM,)),
        ],
        compiler_params=pltpu.CompilerParams(
            collective_id=0, has_side_effects=True, vmem_limit_bytes=48 * 1024 * 1024),
    )(queries, own_kv, cotangent, cartridges, block_mask, owner)


def dispatch(size):
    def run(queries, own_kv, cotangent, cartridges, block_mask, owner):
        fits = (size == 32 and block_mask.shape == (1, 6)
                and queries.shape == (128, QH * HD)
                and cartridges.shape == (1, SLOTS_PER, 2 * KVH * HD))
        chosen = fused if fits else body
        return chosen(queries, own_kv, cotangent, cartridges, block_mask, owner)
    return run


def solution(mesh):
    return jax.shard_map(
        dispatch(mesh.shape["dp"]),
        mesh=mesh,
        in_specs=(
            P(("groups", "dp"), None),
            P(("groups", "dp"), None),
            P(("groups", "dp"), None),
            P(("groups", "dp"), None, None),
            P(("groups", "dp"), None),
            P("groups"),
        ),
        out_specs=P(("groups", "dp"), None),
        check_vma=False,
    )
```

```python
import jax
import jax.numpy as jnp
from jax import lax
from jax.experimental import pallas as pl
from jax.experimental.pallas import tpu as pltpu
from jax.sharding import PartitionSpec as P

HD = 128
QH = 32
KVH = 4
BLOCK = 128


masked_score = -1e30
norm_epsilon = 1e-06


def from_root(value, axis, source):
    kept = jnp.where(lax.axis_index(axis) == source, value, 0).astype(value.dtype)
    return lax.psum(kept, axis)


def head_terms(queries, grad_out, own_keys, own_values, cart_keys, cart_values, allowed, causal):
    score_scale = HD ** (-0.5)
    scores_cart = (
        jnp.einsum("clgd,sd->clgs", queries, cart_keys, preferred_element_type=jnp.float32)
        * score_scale
    )
    scores_own = (
        jnp.einsum("clgd,cud->clgu", queries, own_keys, preferred_element_type=jnp.float32)
        * score_scale
    )
    scores_cart = jnp.where(allowed[:, None, None, :], scores_cart, masked_score)
    scores_own = jnp.where(causal[None, :, None, :], scores_own, masked_score)
    row_max = jnp.maximum(jnp.max(scores_cart, axis=3), jnp.max(scores_own, axis=3))[..., None]
    exp_cart = jnp.exp(scores_cart - row_max)
    exp_own = jnp.exp(scores_own - row_max)
    row_sum = jnp.sum(exp_cart, axis=3, keepdims=True) + jnp.sum(exp_own, axis=3, keepdims=True)
    prob_cart = exp_cart / row_sum
    prob_own = exp_own / row_sum
    low_cart = prob_cart.astype(jnp.bfloat16)
    low_own = prob_own.astype(jnp.bfloat16)
    attended = jnp.einsum(
        "clgs,sd->clgd", low_cart, cart_values, preferred_element_type=jnp.float32
    )
    attended = attended + jnp.einsum(
        "clgu,cud->clgd", low_own, own_values, preferred_element_type=jnp.float32
    )
    grad_prob = jnp.einsum(
        "clgd,sd->clgs", grad_out, cart_values, preferred_element_type=jnp.float32
    )
    row_dot = jnp.sum(grad_out.astype(jnp.float32) * attended, axis=3, keepdims=True)
    grad_score = (prob_cart * (grad_prob - row_dot)).astype(jnp.bfloat16)
    grad_keys = (
        jnp.einsum("clgs,clgd->sd", grad_score, queries, preferred_element_type=jnp.float32)
        * score_scale
    )
    grad_values = jnp.einsum(
        "clgs,clgd->sd", low_cart, grad_out, preferred_element_type=jnp.float32
    )
    return (grad_keys, grad_values)


def body(queries, own_kv, cotangent, cartridges, block_mask, owner):
    conv_dev = block_mask.shape[0]
    seq_len = queries.shape[0] // conv_dev
    slot_count = cartridges.shape[1]
    half_width = KVH * HD
    groups_q = QH // KVH
    owner_index = owner[0]
    local_cart = cartridges[0]
    whole_cart = from_root(local_cart, "dp", owner_index)
    cart_keys = whole_cart[:, :half_width]
    cart_values = whole_cart[:, half_width:]
    query_heads = queries.reshape(conv_dev, seq_len, KVH, groups_q, HD)
    grad_heads = cotangent.reshape(conv_dev, seq_len, KVH, groups_q, HD)
    own_heads = own_kv.reshape(conv_dev, seq_len, 2, KVH, HD)
    key_heads = cart_keys.reshape(slot_count, KVH, HD)
    value_heads = cart_values.reshape(slot_count, KVH, HD)
    allowed = jnp.repeat(block_mask > 0, BLOCK, axis=1)
    positions = jnp.arange(seq_len)
    causal = positions[:, None] >= positions[None, :]
    key_parts = []
    value_parts = []
    for kv_head in range(KVH):
        keys_part, values_part = head_terms(
            query_heads[:, :, kv_head],
            grad_heads[:, :, kv_head],
            own_heads[:, :, 0, kv_head],
            own_heads[:, :, 1, kv_head],
            key_heads[:, kv_head],
            value_heads[:, kv_head],
            allowed,
            causal,
        )
        key_parts.append(keys_part)
        value_parts.append(values_part)
    local_grad = jnp.concatenate(key_parts + value_parts, axis=1)
    width_total = local_grad.shape[1]
    own_rows = lax.psum_scatter(local_grad, "dp", scatter_dimension=0, tiled=True)
    squares = lax.psum(jnp.sum(own_rows * own_rows), "dp")
    return own_rows / jnp.sqrt(squares / (slot_count * width_total) + norm_epsilon)


SCALE = HD ** (-0.5)
LOG2E = 1.4426950408889634


PAIRS = 1
SLICES = 2
LAT = 1.8
COST = 3.0


def attend_begin(j, kv_ref, cart, kk, vv):
    slots = SLOTS_PER
    half = KVH * HD
    kk[:slots] = cart[j, :, :, :, 0].reshape(slots, HD)
    vv[:slots] = cart[j, :, :, :, 1].reshape(slots, HD)
    kk[slots:] = kv_ref[:, j * HD:(j + 1) * HD]
    vv[slots:] = kv_ref[:, half + j * HD:half + (j + 1) * HD]


def attend_slice(j, part, q_ref, ct_ref, bias_ref, kk, vv, acc):
    slots = SLOTS_PER
    groups = QH // KVH
    wide = groups // SLICES // PAIRS * HD
    nt = (((1,), (1,)), ((), ()))
    for i in range(PAIRS):
        base = (j * groups) * HD + (part * PAIRS + i) * wide
        cols = [slice(base + h, base + h + HD) for h in range(0, wide, HD)]
        q = jnp.concatenate([q_ref[:, c] for c in cols], axis=0)
        ct = jnp.concatenate([ct_ref[:, c] for c in cols], axis=0)
        scores = lax.dot_general(kk[...], q, nt, preferred_element_type=jnp.float32)
        x = scores * (SCALE * LOG2E) + bias_ref[:, :wide]
        e = jnp.exp2(x - jnp.max(x, axis=0, keepdims=True))
        prob = e * (1.0 / jnp.sum(e, axis=0, keepdims=True))
        low = prob.astype(jnp.bfloat16)
        gp = lax.dot_general(vv[...], ct, nt, preferred_element_type=jnp.float32)
        row_dot = jnp.sum(low.astype(jnp.float32) * gp, axis=0, keepdims=True)
        gs = (prob[:slots] * (gp[:slots] - row_dot)).astype(jnp.bfloat16)
        gk = jnp.dot(gs, q, preferred_element_type=jnp.float32)
        gv = jnp.dot(low[:slots], ct, preferred_element_type=jnp.float32)
        if part + i == 0:
            acc[:, :HD] = gk
            acc[:, HD:] = gv
        else:
            acc[:, :HD] += gk
            acc[:, HD:] += gv


def attend_end(j, acc, grad):
    for z in range(4):
        for xy in range(4):
            for c in range(2):
                row = 24 * ((z * 4 + xy) * 2 + c)
                to = 24 * ((c * 4 + xy) * 4 + z)
                grad[j, to:to + 24, :HD] = acc[row:row + 24, :HD] * SCALE
                grad[j, to:to + 24, HD:] = acc[row:row + 24, HD:]


SLOTS_PER = 768
SEG = (24, 2 * HD)
N_SEM = 21 * KVH + 10


def kernel(q_hbm, kv_hbm, ct_hbm, cart_hbm, mask_ref, owner_ref, out_ref,
           q_ref, kv_ref, ct_ref, own_cart, load_sem, bias_ref, w_ref, acc, cart, rc, a1, rx, a2, rz, kk, vv, grad,
           gc, b1, sx, gx, b2, gz, own, sq, sqr, send_sem, recv_sem):
    me = lax.axis_index("dp")
    core = me % 2
    xy = (me // 2) % 4
    zz = me // 8
    bit = [me % 2, (me // 2) % 2, (me // 4) % 2, (me // 8) % 2, (me // 16) % 2]
    flip = [1 - 2 * b for b in bit]

    def moved(d, lo):
        step = 0
        if d & 1:
            step = step + flip[lo]
        if d & 2:
            step = step + 2 * flip[lo + 1]
        return step

    core_peer = me + flip[0]
    xy_step = {d: moved(d, 1) for d in (1, 2, 3)}
    z_step = {d: moved(d, 3) for d in (1, 2, 3)}
    xy_peer = {d: me + 2 * xy_step[d] for d in (1, 2, 3)}
    z_peer = {d: me + 8 * z_step[d] for d in (1, 2, 3)}

    staged = [pltpu.make_async_copy(src, dst, load_sem.at[i])
              for i, (src, dst) in enumerate([(cart_hbm, own_cart), (q_hbm, q_ref), (ct_hbm, ct_ref), (kv_hbm, kv_ref)])]
    for copy in staged:
        copy.start()
    barrier = pltpu.get_barrier_semaphore()
    every = {d: me + moved(d % 2, 0) + 2 * moved(d // 2 % 4, 1) + 8 * moved(d // 8, 3) for d in range(1, 32)}
    peers = [every[d] for d in range(1, 8)] + list(z_peer.values())
    for peer in peers:
        pl.semaphore_signal(barrier, inc=1, device_id={"dp": peer}, device_id_type=pl.DeviceIdType.MESH)

    for u in range(0, SLOTS_PER, BLOCK):
        bias_ref[u:u + BLOCK] = jnp.full((BLOCK, bias_ref.shape[1]), jnp.where(mask_ref[0, u // BLOCK] > 0, 0.0, masked_score), jnp.float32)
    own_pos = lax.broadcasted_iota(jnp.int32, (BLOCK, bias_ref.shape[1]), 0)
    row_pos = lax.broadcasted_iota(jnp.int32, (BLOCK, bias_ref.shape[1]), 1) % BLOCK
    bias_ref[SLOTS_PER:] = jnp.where(own_pos <= row_pos, 0.0, masked_score)
    staged[0].wait()
    mine = owner_ref[0] == me
    for j in range(KVH):
        for c in range(2):
            for p in range(4):
                for r in range(2):
                    row = c * 384 + p * 96 + r * 48
                    for v in range(2):
                        col = (v * KVH + j) * HD
                        w_ref[j, c, p, r, v] = jnp.where(mine, own_cart[0, row:row + 48, col:col + HD], 0).astype(jnp.bfloat16)
    pl.semaphore_wait(barrier, len(peers))
    sent = []
    count = [0]

    def send(src, dst, peer):
        i = count[0]
        count[0] += 1
        copy = pltpu.make_async_remote_copy(
            src_ref=src, dst_ref=dst, send_sem=send_sem.at[i], recv_sem=recv_sem.at[i],
            device_id={"dp": peer}, device_id_type=pl.DeviceIdType.MESH)
        copy.start()
        sent.append(copy)
        return copy

    def head(j):
        c = [send(w_ref.at[j, 1 - core], rc.at[j], core_peer)]
        yield ("c", 0.5)
        c[0].wait_recv()
        a1[j] = w_ref[j, core] + rc[j]
        c = [send(a1.at[j, xy + xy_step[d]], rx.at[j, d - 1], xy_peer[d]) for d in (1, 2, 3)]
        yield ("x", 2.0)
        for k in c:
            k.wait_recv()
        a2[j] = (a1[j, xy] + rx[j, 0]) + (rx[j, 1] + rx[j, 2])
        c = []
        for d in (1, 2, 3):
            p = zz + z_step[d]
            c.append(send(a2.at[j, p // 2, p % 2], rz.at[j, d - 1], z_peer[d]))
        yield ("z", 1.0)
        for k in c:
            k.wait_recv()
        spot = cart.at[j, core, xy, zz // 2, zz % 2]
        cart[j, core, xy, zz // 2, zz % 2] = (a2[j, zz // 2, zz % 2] + rz[j, 0]) + (rz[j, 1] + rz[j, 2])
        c = [send(spot, spot, z_peer[d]) for d in (1, 2, 3)]
        yield ("z", 1.0)
        for k in c:
            k.wait_recv()
        spot = cart.at[j, core, xy]
        c = [send(spot, spot, xy_peer[d]) for d in (1, 2, 3)]
        yield ("x", 2.0)
        for k in c:
            k.wait_recv()
        c = [send(cart.at[j, core], cart.at[j, core], core_peer)]
        yield ("c", 0.5)
        c[0].wait_recv()
        yield "compute"
        attend_begin(j, kv_ref, cart, kk, vv)
        for part in range(SLICES):
            attend_slice(j, part, q_ref, ct_ref, bias_ref, kk, vv, acc)
            if part < SLICES - 1:
                yield "compute"
        attend_end(j, acc, grad)
        half = SLOTS_PER // 2
        c = [send(grad.at[j, pl.ds(pl.multiple_of((1 - core) * half, 8), half)], gc.at[j], core_peer)]
        yield ("c", 0.8)
        c[0].wait_recv()
        b1[j] = (grad[j, pl.ds(pl.multiple_of(core * half, 8), half)] + gc[j]).reshape(4, half // 4, 2 * HD)
        c = []
        for d in (1, 2, 3):
            sx[j, d - 1] = b1[j, xy + xy_step[d]].astype(jnp.bfloat16)
            c.append(send(sx.at[j, d - 1], gx.at[j, d - 1], xy_peer[d]))
        yield ("x", 2.0)
        for k in c:
            k.wait_recv()
        total = b1[j, xy]
        for d in (1, 2, 3):
            total = total + gx[j, d - 1].astype(jnp.float32)
        b2[j] = total.reshape(4, SEG[0], SEG[1])
        c = [send(b2.at[j, zz + z_step[d]], gz.at[j, d - 1], z_peer[d]) for d in (1, 2, 3)]
        yield ("z", 2.0)
        for k in c:
            k.wait_recv()
        own[j] = (b2[j, zz] + gz[j, 0]) + (gz[j, 1] + gz[j, 2])

    heads = [head(j) for j in range(KVH)]
    link = {"c": 0.0, "x": 0.0, "z": 0.0}
    now = 0.0
    ready = {}
    computing = []

    def advance(j):
        got = next(heads[j], None)
        ready.pop(j, None)
        if got == "compute":
            computing.append(j)
        elif got is not None:
            name, cost = got
            link[name] = max(link[name], now) + cost
            ready[j] = link[name] + LAT

    for j in range(KVH):
        advance(j)
    for copy in staged[1:]:
        copy.wait()
    while ready or computing:
        arrived = [j for j in sorted(ready) if ready[j] <= now]
        if arrived:
            now += 0.15
            advance(arrived[0])
        elif computing:
            j = min(computing)
            computing.remove(j)
            now += COST / SLICES
            advance(j)
        else:
            now = min(ready.values())

    part = jnp.zeros((8, HD), jnp.float32)
    for j in range(KVH):
        v = own[j]
        v = v * v
        for r in range(0, SEG[0], 8):
            for l in range(0, SEG[1], HD):
                part = part + v[r:r + 8, l:l + HD]
    sq[0] = part
    eight = {d: every[d] for d in range(1, 8)}
    cs = [send(sq.at[0], sqr.at[d - 1], eight[d]) for d in range(1, 8)]
    for k in cs:
        k.wait_recv()
    sq[1] = (((sq[0] + sqr[0]) + (sqr[1] + sqr[2])) + ((sqr[3] + sqr[4]) + (sqr[5] + sqr[6])))
    cs = [send(sq.at[1], sqr.at[6 + d], z_peer[d]) for d in (1, 2, 3)]
    for k in cs:
        k.wait_recv()
    squares = jnp.sum((sq[1] + sqr[7]) + (sqr[8] + sqr[9]))
    factor = 1.0 / jnp.sqrt(squares * jnp.ones((1, HD), jnp.float32) / (SLOTS_PER * 2 * KVH * HD) + norm_epsilon)
    for j in range(KVH):
        out_ref[:, j * HD:(j + 1) * HD] = own[j, :, :HD] * factor
        out_ref[:, (KVH + j) * HD:(KVH + j + 1) * HD] = own[j, :, HD:] * factor
    for k in sent:
        k.wait_send()


def fused(queries, own_kv, cotangent, cartridges, block_mask, owner):
    slots, width = cartridges.shape[1:]
    seq = queries.shape[0]
    bf, f32 = jnp.bfloat16, jnp.float32
    vm = pl.BlockSpec(memory_space=pltpu.VMEM)
    sm = pl.BlockSpec(memory_space=pltpu.SMEM)
    piece = (48, HD)
    return pl.pallas_call(
        kernel,
        out_shape=jax.ShapeDtypeStruct((24, width), f32),
        in_specs=[pl.BlockSpec(memory_space=pltpu.HBM)] * 4 + [sm] * 2,
        out_specs=vm,
        scratch_shapes=[
            pltpu.VMEM(queries.shape, bf),
            pltpu.VMEM(own_kv.shape, bf),
            pltpu.VMEM(cotangent.shape, bf),
            pltpu.VMEM(cartridges.shape, bf),
            pltpu.SemaphoreType.DMA((4,)),
            pltpu.VMEM((slots + seq, QH // KVH // SLICES // PAIRS * HD), f32),
            pltpu.VMEM((KVH, 2, 4, 2, 2) + piece, bf),
            pltpu.VMEM((slots, 2 * HD), f32),
            pltpu.VMEM((KVH, 2, 4, 2, 2) + piece, bf),
            pltpu.VMEM((KVH, 4, 2, 2) + piece, bf),
            pltpu.VMEM((KVH, 4, 2, 2) + piece, bf),
            pltpu.VMEM((KVH, 3, 2, 2) + piece, bf),
            pltpu.VMEM((KVH, 2, 2) + piece, bf),
            pltpu.VMEM((KVH, 3) + piece, bf),
            pltpu.VMEM((slots + seq, HD), bf),
            pltpu.VMEM((slots + seq, HD), bf),
            pltpu.VMEM((KVH, slots, 2 * HD), f32),
            pltpu.VMEM((KVH, slots // 2, 2 * HD), f32),
            pltpu.VMEM((KVH, 4, slots // 8, 2 * HD), f32),
            pltpu.VMEM((KVH, 3, slots // 8, 2 * HD), bf),
            pltpu.VMEM((KVH, 3, slots // 8, 2 * HD), bf),
            pltpu.VMEM((KVH, 4) + SEG, f32),
            pltpu.VMEM((KVH, 3) + SEG, f32),
            pltpu.VMEM((KVH,) + SEG, f32),
            pltpu.VMEM((2, 8, HD), f32),
            pltpu.VMEM((10, 8, HD), f32),
            pltpu.SemaphoreType.DMA((N_SEM,)),
            pltpu.SemaphoreType.DMA((N_SEM,)),
        ],
        compiler_params=pltpu.CompilerParams(
            collective_id=0, has_side_effects=True, vmem_limit_bytes=62 * 1024 * 1024),
    )(queries, own_kv, cotangent, cartridges, block_mask, owner)


def dispatch(size):
    def run(queries, own_kv, cotangent, cartridges, block_mask, owner):
        fits = (size == 32 and block_mask.shape == (1, 6)
                and queries.shape == (128, QH * HD)
                and cartridges.shape == (1, SLOTS_PER, 2 * KVH * HD))
        chosen = fused if fits else body
        return chosen(queries, own_kv, cotangent, cartridges, block_mask, owner)
    return run


def solution(mesh):
    return jax.shard_map(
        dispatch(mesh.shape["dp"]),
        mesh=mesh,
        in_specs=(
            P(("groups", "dp"), None),
            P(("groups", "dp"), None),
            P(("groups", "dp"), None),
            P(("groups", "dp"), None, None),
            P(("groups", "dp"), None),
            P("groups"),
        ),
        out_specs=P(("groups", "dp"), None),
        check_vma=False,
    )
```
